128 devices in a mesh: rows: 32 (over z, x_hi, y), feat: 4 (over x_lo, core).
Axes of the slice: x: 4 (x_hi: 2, x_lo: 2; x = x_hi * 2 + x_lo), y: 4, z: 4, core: 2. Of those that a mesh axis runs over, the one named last changes fastest.
Arguments:
- slab: float32 [16384, 2048], P('rows', 'feat'), may hold values from -42 to 42
- cov_old: float32 [2048, 2048], P('rows', 'feat'), may hold values from -4.5 to 4.5, as said below
Outputs:
- whitened: float32 [16384, 2048], P('rows', 'feat')
- factor: float32 [2048, 2048], P('rows', 'feat')
The draws below stay inside these ranges and needn't reach their ends.
Inputs may be any that keep to these rules, and one draw needn't show every extreme that they name: `cov_old`: symmetric.
All inputs are finite; a program needn't handle non-finite values.
Results may differ from the reference program's by a relative error of at most 0.000098.
Values sent between devices are 32-bit elements; how exact they have to be, the bound alone decides.
A program may use at most 192 MiB of HBM per device.

```python
import math
import jax
import jax.numpy as jnp
from jax import lax

D = 2048
TOTAL = 16384


def draw_slab(key, part):
    key = jax.random.fold_in(key, 11)
    key_noise, key_scale, key_shift = jax.random.split(key, 3)
    row_pos = jnp.arange(TOTAL, dtype=jnp.float32)[:, None]
    rising = 0.5 + row_pos / TOTAL
    col_scale = jnp.exp(jax.random.uniform(key_scale, (1, D), jnp.float32, math.log(0.5), math.log(5.0)))
    shifts = jax.random.uniform(key_shift, (1, D), jnp.float32, -2.0, 2.0)
    noise = jnp.clip(jax.random.normal(key_noise, (TOTAL, D), jnp.float32), -5.0, 5.0)
    return ((noise * col_scale + shifts) * rising).astype(jnp.float32)


def draw_cov_old(key, part):
    key = jax.random.fold_in(key, 23)
    key_off, key_diag = jax.random.split(key)
    entries = jnp.clip(jax.random.normal(key_off, (D, D), jnp.float32), -4.0, 4.0)
    diag_vals = jax.random.uniform(key_diag, (D,), jnp.float32, 2.5, 4.0)
    symmetric = (entries + entries.T) * (0.5 / math.sqrt(D))
    identity = jnp.eye(D, dtype=jnp.float32)
    return (symmetric * (1.0 - identity) + identity * diag_vals[None, :]).astype(jnp.float32)


def setup_inputs(seed: int = 0) -> dict:
    key_list = jax.random.split(jax.random.key(seed), 3)
    slab = draw_slab(jax.random.fold_in(key_list[2], 71), 0)
    cov_old = draw_cov_old(jax.random.fold_in(key_list[2], 71), 0)
    return dict(slab=slab, cov_old=cov_old)


def reference(slab, cov_old):
    means = jnp.sum(slab, axis=0) / TOTAL
    centered = slab - means[None, :]
    gram = lax.dot_general(centered.astype(jnp.float32), centered.astype(jnp.float32), (((0,), (0,)), ((), ())), precision=lax.Precision.HIGHEST, preferred_element_type=jnp.float32)
    covariance = cov_old + gram / TOTAL
    factor = jnp.tril(jnp.linalg.cholesky(covariance))
    whitened = lax.linalg.triangular_solve(factor, centered, left_side=False, lower=True, transpose_a=True)
    return (whitened, factor)
```

```python
import functools
import jax
import jax.numpy as jnp
from jax import lax
from jax.experimental import pallas as pl
from jax.experimental.pallas import tpu as pltpu
from jax.sharding import PartitionSpec as P

F = jnp.float32
BF = jnp.bfloat16


def sbc(x, j):
    return jnp.broadcast_to(x[j : j + 1, :], (8, 128))


def lbc(x, c):
    return jnp.broadcast_to(x[:, c : c + 1], (8, 128))


def split(x):
    h=x.astype(BF); return h,(x-h.astype(F)).astype(BF)
def mm(a,b): return jnp.dot(a,b,preferred_element_type=F)
def diagC(W,vr=2):
    W=list(W)
    lane=lax.broadcasted_iota(jnp.int32,(8,128),1); sub=lax.broadcasted_iota(jnp.int32,(8,128),0)
    us=[];ls=[]
    C=[lbc(W[0],j) for j in range(8)]
    for k in range(16):
        R=W[k]
        g=8*k
        ing=(lane>=g)&(lane<g+8)
        X=jnp.where(ing,jnp.where(lane-g==sub,1.0,0.0),R); V=R
        FX=X; FV=V
        pv=jnp.ones((8,128),F)
        nxt=k<15
        if nxt:
            Q=[lbc(W[k+1],g+c) for c in range(16)]
            Q0=Q[:8]
        for j in range(0,8,2):
            a=sbc(C[j],j); b=sbc(C[j],j+1); d=sbc(C[j+1],j+1)
            det=a*d-b*b
            rd=1.0/det
            c0=C[j]; c1=C[j+1]
            s0=sub==j; s1=sub==j+1; sp=s0|s1
            n0=jnp.where(s0,-d,jnp.where(s1,b,c0*d-c1*b)); n1=jnp.where(s0,b,jnp.where(s1,-a,c1*a-c0*b))
            m0=n0*rd; m1=n1*rd
            if nxt:
                q0=Q[j]; q1=Q[j+1]
                h0=(q0*d-q1*b)*rd; h1=(q1*a-q0*b)*rd
            def upd(q):
                r0=sbc(q,j); r1=sbc(q,j+1)
                return jnp.where(sp,0.0,q)-(m0*r0+m1*r1), r0, r1
            for c in range(j+2,8):
                C[c],r0,r1=upd(C[c])
                if nxt: Q[c]=Q[c]-(h0*r0+h1*r1)
            if nxt:
                for c in range(8):
                    Q[8+c]=Q[8+c]-(h0*sbc(q0,c)+h1*sbc(q1,c))
            ba=b/a
            X,r0,r1=upd(X)
            FX=jnp.where(s0,r0,jnp.where(s1,r1-ba*r0,FX))
            V,r0,r1=upd(V)
            FV=jnp.where(s0,r0,jnp.where(s1,r1-ba*r0,FV))
            pv=jnp.where(s0,a,jnp.where(s1,d-ba*b,pv))
        Z=X; rs=lax.rsqrt(pv)
        us.append(jnp.where(lane>=g+sub,FV*rs,0.0)); ls.append(jnp.where(lane<=g+sub,FX*rs,0.0))
        zb=[sbc(Z,j) for j in range(8)]
        if nxt: C=Q[8:]
        for i in range(k+1,min(k+1+vr,16)):
            acc=jnp.where(ing,0.0,W[i])
            for j in range(8):
                acc=acc-(Q0[j] if i==k+1 else lbc(W[i],g+j))*zb[j]
            W[i]=acc
        lo=k+1+vr
        if lo<16:
            Wt=jnp.concatenate(W[lo:],axis=0); wh,wl=split(Wt)
            zz=[jnp.zeros((8*k,128),F)] if k else []
            Zf=jnp.concatenate(zz+[Z,jnp.zeros((120-8*k,128),F)],axis=0)
            zh,zl=split(Zf)
            D=mm(wh,zh)+(mm(wh,zl)+mm(wl,zh))
            for i in range(lo,16):
                W[i]=jnp.where(ing,0.0,W[i])-D[8*(i-lo):8*(i-lo)+8]
    return us,ls

BLK={(1,0):0,(2,0):1,(3,0):2,(2,1):3,(3,1):4,(3,2):5}
def nt(a,b): return lax.dot_general(a,b,(((1,),(1,)),((),())),preferred_element_type=F)
def nt3(ah,al,bh,bl): return nt(ah,bh)+(nt(ah,bl)+nt(al,bh))
def nn3(ah,al,bh,bl): return mm(ah,bh)+(mm(ah,bl)+mm(al,bh))
def gtile(g_ref,I,J,t):
    if I==J: return g_ref[J,pl.ds(16*t,16),0:16,:].reshape(256,512)
    if (I,J)==(3,0): return g_ref[3,pl.ds(16*t,16),16:32,:].reshape(256,512)
    if I==J+1: return g_ref[J,pl.ds(16*t,16),16:32,:].reshape(256,512)
    return g_ref[J+2*t,:,32:40,:].reshape(256,512)
def k3(s_ref,g_ref,c_ref,y_ref,f_ref,S,UR,XH,XL,LF,LH,LL,YH,YL):
    f=s_ref[0]; blk=s_ref[1]; sb=s_ref[2]
    for J in range(4):
        @pl.loop(0,2)
        def _(t):
            acc=gtile(g_ref,J,J,t)
            rows=pl.ds(pl.multiple_of(256*t,256),256)
            for K in range(J):
                q=BLK[(J,K)]
                acc=acc-nt3(LH[q,rows,:],LL[q,rows,:],LH[q],LL[q])
            for u in range(2):
                for c in range(4):
                    S[2*t+u,c]=acc[128*u:128*u+128,128*c:128*c+128]
        lane=lax.broadcasted_iota(jnp.int32,(128,128),1); row=lax.broadcasted_iota(jnp.int32,(128,128),0)
        @pl.loop(0,4)
        def _(b):
            D=S[b,b]
            us,ls=diagC([D[8*k:8*k+8] for k in range(16)])
            li=jnp.concatenate(ls,axis=0)
            LF[J,J,b,b]=jnp.concatenate(us,axis=0).T
            S[b,b]=jnp.where(lane==row,1.0,0.0)
            lh,ll=split(li)
            rr=jnp.concatenate([S[b,c] for c in range(4)],axis=1)
            rh,rl=split(rr)
            ur=nn3(lh,ll,rh,rl)
            for c in range(4):
                UR[b,c]=jnp.where(c<=b,ur[:,128*c:128*c+128],0.0)
            uh,ul=split(ur)
            @pl.loop(b+1,4)
            def _(i):
                ph,plo=split(S[i,b])
                p=nt3(ph,plo,lh,ll)
                LF[J,J,i,b]=p
                LF[J,J,b,i]=jnp.zeros((128,128),F)
                S[i,b]=jnp.zeros((128,128),F)
                ph,plo=split(p)
                d=nn3(ph,plo,uh,ul)
                for c in range(4):
                    S[i,c]=S[i,c]-d[:,128*c:128*c+128]
        for b in range(4):
            x=jnp.concatenate([UR[b,c] for c in range(4)],axis=1)
            h,l=split(x)
            XH[128*b:128*b+128,:]=h; XL[128*b:128*b+128,:]=l
        for I in range(J+1,4):
            @pl.loop(0,2)
            def _(t):
                acc=gtile(g_ref,I,J,t)
                rows=pl.ds(pl.multiple_of(256*t,256),256)
                for K in range(J):
                    q=BLK[(I,K)]; w=BLK[(J,K)]
                    acc=acc-nt3(LH[q,rows,:],LL[q,rows,:],LH[w],LL[w])
                ah,al=split(acc)
                p=nt3(ah,al,XH[...],XL[...])
                for u in range(2):
                    for c in range(4):
                        LF[I,J,2*t+u,c]=p[128*u:128*u+128,128*c:128*c+128]
                h,l=split(p)
                q=BLK[(I,J)]
                LH[q,rows,:]=h; LL[q,rows,:]=l
        @pl.when(f>=J)
        def _():
            @pl.loop(0,2)
            def _(t):
                rows=pl.ds(pl.multiple_of(256*t,256),256)
                acc=c_ref[J,rows,:]
                for K in range(J):
                    w=BLK[(J,K)]
                    acc=acc-nt3(YH[K,rows,:],YL[K,rows,:],LH[w],LL[w])
                ah,al=split(acc)
                p=nt3(ah,al,XH[...],XL[...])
                y_ref[rows,:]=p
                if J<3:
                    h,l=split(p)
                    YH[J,rows,:]=h; YL[J,rows,:]=l
    half=pl.ds(pl.multiple_of(64*(sb%2),64),64)
    for c in range(4):
        f_ref[:,128*c:128*c+128]=jnp.where(blk>=f,LF[blk,f,sb//2,c,half,:],0.0)
def k3call(s,g,c):
    V=pltpu.VMEM
    return pl.pallas_call(k3,out_shape=[jax.ShapeDtypeStruct((512,512),F),jax.ShapeDtypeStruct((64,512),F)],
        in_specs=[pl.BlockSpec(memory_space=pltpu.SMEM),pl.BlockSpec(memory_space=V),pl.BlockSpec(memory_space=V)],
        out_specs=[pl.BlockSpec(memory_space=V)]*2,
        scratch_shapes=[V((4,4,128,128),F),V((4,4,128,128),F),V((512,512),BF),V((512,512),BF),V((4,4,4,4,128,128),F),
            V((6,512,512),BF),V((6,512,512),BF),V((3,512,512),BF),V((3,512,512),BF)],
        compiler_params=pltpu.CompilerParams(vmem_limit_bytes=60*2**20))(s,g,c)


def dot_t(a, b):
    return lax.dot_general(
        a, b, (((0,), (0,)), ((), ())), precision=lax.Precision.HIGHEST, preferred_element_type=F
    )


def per_device(slab, cov_old):
    n_rows = lax.axis_size("rows")
    r = lax.axis_index("rows")
    f = lax.axis_index("feat")
    rows_dev, width = slab.shape
    total = rows_dev * n_rows
    blk = r // 8
    sub = r % 8
    sums = lax.psum(jnp.sum(slab, axis=0), "rows")
    centered = slab - (sums / total)[None, :]
    c = lax.all_gather(centered, "feat", axis=0)
    pick = lambda i: lax.dynamic_index_in_dim(c, i, 0, keepdims=False)
    o_row = jnp.minimum(f + 1, 3)
    o_col = jnp.where(f < 3, f, 0)
    h_row = jnp.where(f < 2, f + 2, f)
    h_col = jnp.where(f < 2, f, f - 2)
    h_low = jnp.where(f < 2, 0, 256)
    left_h = lax.dynamic_slice_in_dim(pick(h_row), h_low, 256, 1)
    base = lax.dynamic_update_slice_in_dim(jnp.zeros((512, 512), F), cov_old, 64 * sub, 0)
    base_t = base.T
    zero = jnp.zeros((), F)
    d = dot_t(centered, centered) / total + jnp.where(blk == f, base, zero)
    o = dot_t(pick(o_row), pick(o_col)) / total
    o += jnp.where(f < 3, jnp.where(blk == f + 1, base, zero), jnp.where(blk == 0, base_t, zero))
    h = dot_t(left_h, pick(h_col)) / total
    h += jnp.where(
        f < 2,
        jnp.where(blk == f + 2, base[:256], zero),
        jnp.where(blk == f - 2, base_t[256:], zero),
    )
    parts = jnp.concatenate(
        [d.reshape(32, 16, 512), o.reshape(32, 16, 512), h.reshape(32, 8, 512)], axis=1
    )
    mine = lax.psum_scatter(parts, "rows", scatter_dimension=0, tiled=False)
    g = lax.all_gather(mine, "rows", axis=0)
    g = lax.all_gather(g, "feat", axis=0)
    s = jnp.stack([f, blk, sub]).astype(jnp.int32)
    y, fac = k3call(s, g, c)
    return (y, fac)


def solution(mesh):
    placed = (P("rows", "feat"), P("rows", "feat"))
    return jax.shard_map(
        per_device, mesh=mesh, in_specs=placed, out_specs=placed, check_vma=False
    )
```

```python
import functools
import jax
import jax.numpy as jnp
from jax import lax
from jax.experimental import pallas as pl
from jax.experimental.pallas import tpu as pltpu
from jax.sharding import PartitionSpec as P

F = jnp.float32
BF = jnp.bfloat16


def sbc(x, j):
    return jnp.broadcast_to(x[j : j + 1, :], (8, 128))


def lbc(x, c):
    return jnp.broadcast_to(x[:, c : c + 1], (8, 128))


def split(x):
    h=x.astype(BF); return h,(x-h.astype(F)).astype(BF)
def mm(a,b): return jnp.dot(a,b,preferred_element_type=F)
def diagC(W,vr=2):
    W=list(W)
    lane=lax.broadcasted_iota(jnp.int32,(8,128),1); sub=lax.broadcasted_iota(jnp.int32,(8,128),0)
    us=[];ls=[]
    C=[lbc(W[0],j) for j in range(8)]
    for k in range(16):
        R=W[k]
        g=8*k
        ing=(lane>=g)&(lane<g+8)
        X=jnp.where(ing,jnp.where(lane-g==sub,1.0,0.0),R); V=R
        FX=X; FV=V
        pv=jnp.ones((8,128),F)
        nxt=k<15
        if nxt:
            Q=[lbc(W[k+1],g+c) for c in range(16)]
            Q0=Q[:8]
        for j in range(0,8,2):
            a=sbc(C[j],j); b=sbc(C[j],j+1); d=sbc(C[j+1],j+1)
            det=a*d-b*b
            rd=1.0/det
            c0=C[j]; c1=C[j+1]
            s0=sub==j; s1=sub==j+1; sp=s0|s1
            n0=jnp.where(s0,-d,jnp.where(s1,b,c0*d-c1*b)); n1=jnp.where(s0,b,jnp.where(s1,-a,c1*a-c0*b))
            m0=n0*rd; m1=n1*rd
            if nxt:
                q0=Q[j]; q1=Q[j+1]
                h0=(q0*d-q1*b)*rd; h1=(q1*a-q0*b)*rd
            def upd(q):
                r0=sbc(q,j); r1=sbc(q,j+1)
                return jnp.where(sp,0.0,q)-(m0*r0+m1*r1), r0, r1
            for c in range(j+2,8):
                C[c],r0,r1=upd(C[c])
                if nxt: Q[c]=Q[c]-(h0*r0+h1*r1)
            if nxt:
                for c in range(8):
                    Q[8+c]=Q[8+c]-(h0*sbc(q0,c)+h1*sbc(q1,c))
            ba=b/a
            X,r0,r1=upd(X)
            FX=jnp.where(s0,r0,jnp.where(s1,r1-ba*r0,FX))
            V,r0,r1=upd(V)
            FV=jnp.where(s0,r0,jnp.where(s1,r1-ba*r0,FV))
            pv=jnp.where(s0,a,jnp.where(s1,d-ba*b,pv))
        Z=X; rs=lax.rsqrt(pv)
        us.append(jnp.where(lane>=g+sub,FV*rs,0.0)); ls.append(jnp.where(lane<=g+sub,FX*rs,0.0))
        zb=[sbc(Z,j) for j in range(8)]
        if nxt: C=Q[8:]
        for i in range(k+1,min(k+1+vr,16)):
            acc=jnp.where(ing,0.0,W[i])
            for j in range(8):
                acc=acc-(Q0[j] if i==k+1 else lbc(W[i],g+j))*zb[j]
            W[i]=acc
        lo=k+1+vr
        if lo<16:
            Wt=jnp.concatenate(W[lo:],axis=0); wh,wl=split(Wt)
            zz=[jnp.zeros((8*k,128),F)] if k else []
            Zf=jnp.concatenate(zz+[Z,jnp.zeros((120-8*k,128),F)],axis=0)
            zh,zl=split(Zf)
            D=mm(wh,zh)+(mm(wh,zl)+mm(wl,zh))
            for i in range(lo,16):
                W[i]=jnp.where(ing,0.0,W[i])-D[8*(i-lo):8*(i-lo)+8]
    return us,ls

BLK={(1,0):0,(2,0):1,(3,0):2,(2,1):3,(3,1):4,(3,2):5}
def nt(a,b): return lax.dot_general(a,b,(((1,),(1,)),((),())),preferred_element_type=F)
def nt3(ah,al,bh,bl): return nt(ah,bh)+(nt(ah,bl)+nt(al,bh))
def nn3(ah,al,bh,bl): return mm(ah,bh)+(mm(ah,bl)+mm(al,bh))
def gtile(g_ref,I,J,t):
    if I==J: return g_ref[J,pl.ds(16*t,16),0:16,:].reshape(256,512)
    if (I,J)==(3,0): return g_ref[3,pl.ds(16*t,16),16:32,:].reshape(256,512)
    if I==J+1: return g_ref[J,pl.ds(16*t,16),16:32,:].reshape(256,512)
    return g_ref[J+2*t,:,32:40,:].reshape(256,512)
def k3(s_ref,g_ref,c_ref,y_ref,f_ref,S,UR,XH,XL,LF,LH,LL,YH,YL):
    f=s_ref[0]; blk=s_ref[1]; sb=s_ref[2]
    for J in range(4):
        @pl.loop(0,2)
        def _(t):
            acc=gtile(g_ref,J,J,t)
            rows=pl.ds(pl.multiple_of(256*t,256),256)
            for K in range(J):
                q=BLK[(J,K)]
                acc=acc-nt3(LH[q,rows,:],LL[q,rows,:],LH[q],LL[q])
            for u in range(2):
                for c in range(4):
                    S[2*t+u,c]=acc[128*u:128*u+128,128*c:128*c+128]
        lane=lax.broadcasted_iota(jnp.int32,(128,128),1); row=lax.broadcasted_iota(jnp.int32,(128,128),0)
        @pl.loop(0,4)
        def _(b):
            D=S[b,b]
            us,ls=diagC([D[8*k:8*k+8] for k in range(16)])
            li=jnp.concatenate(ls,axis=0)
            LF[J,J,b,b]=jnp.concatenate(us,axis=0).T
            S[b,b]=jnp.where(lane==row,1.0,0.0)
            lh,ll=split(li)
            rr=jnp.concatenate([S[b,c] for c in range(4)],axis=1)
            rh,rl=split(rr)
            ur=nn3(lh,ll,rh,rl)
            for c in range(4):
                UR[b,c]=jnp.where(c<=b,ur[:,128*c:128*c+128],0.0)
            uh,ul=split(ur)
            @pl.loop(b+1,4)
            def _(i):
                ph,plo=split(S[i,b])
                p=nt3(ph,plo,lh,ll)
                LF[J,J,i,b]=p
                LF[J,J,b,i]=jnp.zeros((128,128),F)
                S[i,b]=jnp.zeros((128,128),F)
                ph,plo=split(p)
                d=nn3(ph,plo,uh,ul)
                for c in range(4):
                    S[i,c]=S[i,c]-d[:,128*c:128*c+128]
        for b in range(4):
            x=jnp.concatenate([UR[b,c] for c in range(4)],axis=1)
            h,l=split(x)
            XH[128*b:128*b+128,:]=h; XL[128*b:128*b+128,:]=l
        for I in range(J+1,4):
            @pl.loop(0,2)
            def _(t):
                acc=gtile(g_ref,I,J,t)
                rows=pl.ds(pl.multiple_of(256*t,256),256)
                for K in range(J):
                    q=BLK[(I,K)]; w=BLK[(J,K)]
                    acc=acc-nt3(LH[q,rows,:],LL[q,rows,:],LH[w],LL[w])
                ah,al=split(acc)
                p=nt3(ah,al,XH[...],XL[...])
                for u in range(2):
                    for c in range(4):
                        LF[I,J,2*t+u,c]=p[128*u:128*u+128,128*c:128*c+128]
                h,l=split(p)
                q=BLK[(I,J)]
                LH[q,rows,:]=h; LL[q,rows,:]=l
        @pl.when(f>=J)
        def _():
            @pl.loop(0,2)
            def _(t):
                rows=pl.ds(pl.multiple_of(256*t,256),256)
                acc=c_ref[J,rows,:]
                for K in range(J):
                    w=BLK[(J,K)]
                    acc=acc-nt3(YH[K,rows,:],YL[K,rows,:],LH[w],LL[w])
                ah,al=split(acc)
                p=nt3(ah,al,XH[...],XL[...])
                y_ref[rows,:]=p
                if J<3:
                    h,l=split(p)
                    YH[J,rows,:]=h; YL[J,rows,:]=l
    half=pl.ds(pl.multiple_of(64*(sb%2),64),64)
    for c in range(4):
        f_ref[:,128*c:128*c+128]=jnp.where(blk>=f,LF[blk,f,sb//2,c,half,:],0.0)
def k3call(s,g,c):
    V=pltpu.VMEM
    return pl.pallas_call(k3,out_shape=[jax.ShapeDtypeStruct((512,512),F),jax.ShapeDtypeStruct((64,512),F)],
        in_specs=[pl.BlockSpec(memory_space=pltpu.SMEM),pl.BlockSpec(memory_space=V),pl.BlockSpec(memory_space=V)],
        out_specs=[pl.BlockSpec(memory_space=V)]*2,
        scratch_shapes=[V((4,4,128,128),F),V((4,4,128,128),F),V((512,512),BF),V((512,512),BF),V((4,4,4,4,128,128),F),
            V((6,512,512),BF),V((6,512,512),BF),V((3,512,512),BF),V((3,512,512),BF)],
        compiler_params=pltpu.CompilerParams(vmem_limit_bytes=60*2**20))(s,g,c)


MESH = pl.DeviceIdType.MESH


def remote(src, dst, send, recv, rows, feat):
    return pltpu.make_async_remote_copy(
        src_ref=src, dst_ref=dst, send_sem=send, recv_sem=recv,
        device_id=(rows, feat), device_id_type=MESH,
    )


def greet(peers):
    barrier = pltpu.get_barrier_semaphore()
    for rows, feat in peers:
        pl.semaphore_signal(barrier, inc=1, device_id=(rows, feat), device_id_type=MESH)
    pl.semaphore_wait(barrier, len(peers))


def gather_kernel(slab, c, m, sums, own, s_send, s_recv, m_send, m_recv, x_send, x_recv, b_send, b_recv, f_send, f_recv):
    r = lax.axis_index("rows")
    f = lax.axis_index("feat")
    core = f % 2
    side = f // 2
    sib = 2 * side + 1 - core
    opp = 2 * (1 - side) + core
    feats = [(f + d) % 4 for d in range(1, 4)]
    greet([((r + d) % 32, f) for d in range(1, 32)] + [(r, g) for g in feats])
    across = []
    for q in range(4):
        part = pl.ds(128 * q, 128)
        cp = remote(slab.at[part], c.at[f, part], x_send.at[q], x_recv.at[q], r, opp)
        cp.start()
        across.append(cp)
    beside = remote(slab, c.at[f], b_send, b_recv, r, sib)
    beside.start()
    keep = pltpu.make_async_copy(slab, c.at[f], own)
    keep.start()
    sums[r] = jnp.sum(slab[...], axis=0, keepdims=True)
    sent = []
    for d in range(1, 32):
        cp = remote(sums.at[r], sums.at[r], s_send.at[d], s_recv.at[d], (r + d) % 32, f)
        cp.start()
        sent.append(cp)
    for cp in sent:
        cp.wait_recv()
    m[f] = jnp.sum(sums[...], axis=0) * (1.0 / 16384.0)
    shared = []
    for d in range(1, 4):
        cp = remote(m.at[f], m.at[f], m_send.at[d], m_recv.at[d], r, (f + d) % 4)
        cp.start()
        shared.append(cp)
    passed = []
    for q in range(4):
        part = pl.ds(128 * q, 128)
        across[q].wait_recv()
        cp = remote(c.at[opp, part], c.at[opp, part], f_send.at[q], f_recv.at[q], r, sib)
        cp.start()
        passed.append(cp)
    for cp in sent + across:
        cp.wait_send()
    for cp in shared + passed + [beside, keep]:
        cp.wait()


def gather(slab):
    D = pltpu.SemaphoreType.DMA
    V = pltpu.VMEM
    return pl.pallas_call(
        gather_kernel,
        out_shape=[jax.ShapeDtypeStruct((4, 512, 512), F), jax.ShapeDtypeStruct((4, 1, 512), F)],
        in_specs=[pl.BlockSpec(memory_space=V)],
        out_specs=[pl.BlockSpec(memory_space=V)] * 2,
        scratch_shapes=[V((32, 1, 512), F), D(()), D((32,)), D((32,)), D((4,)), D((4,)), D((4,)), D((4,)), D(()), D(()), D((4,)), D((4,))],
        compiler_params=pltpu.CompilerParams(collective_id=1, has_side_effects=True, vmem_limit_bytes=24 * 2**20),
    )(slab)


PIECE = ((0, 16), (16, 16), (32, 8))
ORDER = (("y", "z", "x"), ("z", "x", "y"), ("x", "y", "z"))


def reduce_kernel(parts, g, inbox, mine, p_send, p_recv, own, a_send, a_recv, c_send, c_recv):
    r = lax.axis_index("rows")
    f = lax.axis_index("feat")
    core = f % 2
    at = {"z": r // 8, "x": 2 * ((r // 4) % 2) + f // 2, "y": r % 4}

    def place(pos, cr):
        return (pos["z"] * 2 + pos["x"] // 2) * 4 + pos["y"], (pos["x"] % 2) * 2 + cr

    def moved(dim, by):
        pos = dict(at)
        pos[dim] = (at[dim] + by + 4) % 4
        return pos

    sib = place(at, 1 - core)
    greet([((r + d) % 32, f) for d in range(1, 32)] + [place(moved("x", 1), core), place(moved("x", -1), core), sib])
    sent = []
    for d in range(1, 32):
        to = (r + d) % 32
        cp = remote(parts.at[to], inbox.at[d], p_send.at[d], p_recv.at[d], to, f)
        cp.start()
        sent.append(cp)
    for cp in sent:
        cp.wait_recv()
    total = parts[r]
    for d in range(1, 32):
        total = total + inbox[d]
    mine[...] = total

    def view(ref, piece, pos, full, lanes=(0, 512)):
        a, n = PIECE[piece]
        every = pl.ds(0, 4)
        two = pl.ds(0, 2)
        xl = two if "x" in full else pos["x"] % 2
        xh = two if "x" in full else pos["x"] // 2
        zz = every if "z" in full else pos["z"]
        yy = every if "y" in full else pos["y"]
        return ref.at[xl, core, zz, xh, yy, pl.ds(a, n), pl.ds(lanes[0], lanes[1])]

    pending = []
    count = [0]

    def pass_on(piece, pos, full):
        k = count[0]
        count[0] += 1
        v = view(g, piece, pos, full)
        cp = remote(v, v, c_send.at[k], c_recv.at[k], *sib)
        cp.start()
        pending.append(cp)

    for p in range(3):
        a, n = PIECE[p]
        cp = pltpu.make_async_copy(mine.at[pl.ds(a, n)], view(g, p, at, ()), own.at[p])
        cp.start()
        cp.wait()
    for s in range(3):
        first = []
        for p in range(3):
            dim = ORDER[p][s]
            full = ORDER[p][:s]
            v = view(g, p, at, full)
            pair = []
            for way, by in enumerate((1, -1)):
                k = (p * 3 + s) * 4 + way
                cp = remote(v, v, a_send.at[k], a_recv.at[k], *place(moved(dim, by), core))
                cp.start()
                pair.append(cp)
            first.append(pair)
            if s == 0:
                pass_on(p, at, ())
        second = []
        for p in range(3):
            dim = ORDER[p][s]
            full = ORDER[p][:s]
            pair = []
            for way, by in enumerate((1, -1)):
                first[p][way].wait_recv()
                k = (p * 3 + s) * 4 + 2 + way
                v = view(g, p, moved(dim, -by), full, (256 * way, 256))
                cp = remote(v, v, a_send.at[k], a_recv.at[k], *place(moved(dim, by), core))
                cp.start()
                pair.append(cp)
            second.append(pair)
            for by in (-1, 1):
                pass_on(p, moved(dim, by), full)
        for p in range(3):
            for cp in second[p]:
                cp.wait_recv()
            pass_on(p, moved(ORDER[p][s], 2), ORDER[p][:s])
            for cp in first[p] + second[p]:
                cp.wait_send()
    for cp in pending:
        cp.wait()
    for cp in sent:
        cp.wait_send()


def reduce_gather(parts):
    D = pltpu.SemaphoreType.DMA
    V = pltpu.VMEM
    return pl.pallas_call(
        reduce_kernel,
        out_shape=jax.ShapeDtypeStruct((2, 2, 4, 2, 4, 40, 512), F),
        in_specs=[pl.BlockSpec(memory_space=V)],
        out_specs=pl.BlockSpec(memory_space=pl.ANY),
        scratch_shapes=[V((32, 40, 512), F), V((40, 512), F), D((32,)), D((32,)), D((3,)), D((36,)), D((36,)), D((30,)), D((30,))],
        compiler_params=pltpu.CompilerParams(collective_id=2, has_side_effects=True, vmem_limit_bytes=24 * 2**20),
    )(parts)


def dot_t(a, b):
    return lax.dot_general(
        a, b, (((0,), (0,)), ((), ())), precision=lax.Precision.HIGHEST, preferred_element_type=F
    )


def per_device(slab, cov_old):
    n_rows = lax.axis_size("rows")
    r = lax.axis_index("rows")
    f = lax.axis_index("feat")
    rows_dev, width = slab.shape
    total = rows_dev * n_rows
    blk = r // 8
    sub = r % 8
    raw, means = gather(slab)
    c = raw - means
    pick = lambda i: lax.dynamic_index_in_dim(c, i, 0, keepdims=False)
    o_row = jnp.minimum(f + 1, 3)
    o_col = jnp.where(f < 3, f, 0)
    h_row = jnp.where(f < 2, f + 2, f)
    h_col = jnp.where(f < 2, f, f - 2)
    h_low = jnp.where(f < 2, 0, 256)
    left_h = lax.dynamic_slice_in_dim(pick(h_row), h_low, 256, 1)
    base = lax.dynamic_update_slice_in_dim(jnp.zeros((512, 512), F), cov_old, 64 * sub, 0)
    base_t = base.T
    zero = jnp.zeros((), F)
    centered = pick(f)
    d = dot_t(centered, centered) / total + jnp.where(blk == f, base, zero)
    o = dot_t(pick(o_row), pick(o_col)) / total
    o += jnp.where(f < 3, jnp.where(blk == f + 1, base, zero), jnp.where(blk == 0, base_t, zero))
    h = dot_t(left_h, pick(h_col)) / total
    h += jnp.where(
        f < 2,
        jnp.where(blk == f + 2, base[:256], zero),
        jnp.where(blk == f - 2, base_t[256:], zero),
    )
    parts = jnp.concatenate(
        [d.reshape(32, 16, 512), o.reshape(32, 16, 512), h.reshape(32, 8, 512)], axis=1
    )
    g = reduce_gather(parts).reshape(4, 32, 40, 512)
    s = jnp.stack([f, blk, sub]).astype(jnp.int32)
    y, fac = k3call(s, g, c)
    return (y, fac)


def solution(mesh):
    placed = (P("rows", "feat"), P("rows", "feat"))
    return jax.shard_map(
        per_device, mesh=mesh, in_specs=placed, out_specs=placed, check_vma=False
    )
```

```python
import functools
import jax
import jax.numpy as jnp
from jax import lax
from jax.experimental import pallas as pl
from jax.experimental.pallas import tpu as pltpu
from jax.sharding import PartitionSpec as P

F = jnp.float32
BF = jnp.bfloat16


def sbc(x, j):
    return jnp.broadcast_to(x[j : j + 1, :], (8, 128))


def lbc(x, c):
    return jnp.broadcast_to(x[:, c : c + 1], (8, 128))


BF=jnp.bfloat16
def split(x):
    h=x.astype(BF); return h,(x-h.astype(F)).astype(BF)
def mm(a,b): return jnp.dot(a,b,preferred_element_type=F)
def diagC(W,side=(),vr=2):
    W=list(W)
    lane=lax.broadcasted_iota(jnp.int32,(8,128),1); sub=lax.broadcasted_iota(jnp.int32,(8,128),0)
    us=[];ls=[]
    C=[lbc(W[0],j) for j in range(8)]
    for k in range(16):
        for q in side[k::16]: q()
        R=W[k]
        g=8*k
        ing=(lane>=g)&(lane<g+8)
        X=jnp.where(ing,jnp.where(lane-g==sub,1.0,0.0),R); V=R
        FX=X; FV=V
        pv=jnp.ones((8,128),F)
        nxt=k<15
        if nxt:
            Q=[lbc(W[k+1],g+c) for c in range(16)]
            Q0=Q[:8]
        for j in range(0,8,2):
            a=sbc(C[j],j); b=sbc(C[j],j+1); d=sbc(C[j+1],j+1)
            det=a*d-b*b
            rd=1.0/det
            c0=C[j]; c1=C[j+1]
            s0=sub==j; s1=sub==j+1; sp=s0|s1
            n0=jnp.where(s0,-d,jnp.where(s1,b,c0*d-c1*b)); n1=jnp.where(s0,b,jnp.where(s1,-a,c1*a-c0*b))
            m0=n0*rd; m1=n1*rd
            if nxt:
                q0=Q[j]; q1=Q[j+1]
                h0=(q0*d-q1*b)*rd; h1=(q1*a-q0*b)*rd
            def upd(q):
                r0=sbc(q,j); r1=sbc(q,j+1)
                return jnp.where(sp,0.0,q)-(m0*r0+m1*r1), r0, r1
            for c in range(j+2,8):
                C[c],r0,r1=upd(C[c])
                if nxt: Q[c]=Q[c]-(h0*r0+h1*r1)
            if nxt:
                for c in range(8):
                    Q[8+c]=Q[8+c]-(h0*sbc(q0,c)+h1*sbc(q1,c))
            ba=b/a
            X,r0,r1=upd(X)
            FX=jnp.where(s0,r0,jnp.where(s1,r1-ba*r0,FX))
            V,r0,r1=upd(V)
            FV=jnp.where(s0,r0,jnp.where(s1,r1-ba*r0,FV))
            pv=jnp.where(s0,a,jnp.where(s1,d-ba*b,pv))
        Z=X; rs=lax.rsqrt(pv)
        us.append(jnp.where(lane>=g+sub,FV*rs,0.0)); ls.append(jnp.where(lane<=g+sub,FX*rs,0.0))
        zb=[sbc(Z,j) for j in range(8)]
        if nxt: C=Q[8:]
        for i in range(k+1,min(k+1+vr,16)):
            acc=jnp.where(ing,0.0,W[i])
            for j in range(8):
                acc=acc-(Q0[j] if i==k+1 else lbc(W[i],g+j))*zb[j]
            W[i]=acc
        lo=k+1+vr
        if lo<16:
            Wt=jnp.concatenate(W[lo:],axis=0); wh,wl=split(Wt)
            zz=[jnp.zeros((8*k,128),F)] if k else []
            Zf=jnp.concatenate(zz+[Z,jnp.zeros((120-8*k,128),F)],axis=0)
            zh,zl=split(Zf)
            D=mm(wh,zh)+(mm(wh,zl)+mm(wl,zh))
            for i in range(lo,16):
                W[i]=jnp.where(ing,0.0,W[i])-D[8*(i-lo):8*(i-lo)+8]
    return us,ls

BLK={(1,0):0,(2,0):1,(3,0):2,(2,1):3,(3,1):4,(3,2):5}
AX={(2,1):0,(3,1):1,(3,2):2}
def tri(i,j): return i*(i+1)//2+j
def nt(a,b): return lax.dot_general(a,b,(((1,),(1,)),((),())),preferred_element_type=F)
def nt3(ah,al,bh,bl): return nt(ah,bh)+(nt(ah,bl)+nt(al,bh))
def nn3(ah,al,bh,bl): return mm(ah,bh)+(mm(ah,bl)+mm(al,bh))
def gtile(g_ref,I,J,t):
    if I==J: return g_ref[J,pl.ds(16*t,16),0:16,:].reshape(256,512)
    if (I,J)==(3,0): return g_ref[3,pl.ds(16*t,16),16:32,:].reshape(256,512)
    if I==J+1: return g_ref[J,pl.ds(16*t,16),16:32,:].reshape(256,512)
    return g_ref[J+2*t,:,32:40,:].reshape(256,512)
def rws(t): return pl.ds(pl.multiple_of(256*t,256),256)
def k3(s_ref,g_hbm,c_hbm,y_ref,f_ref,g_ref,c_ref,sem,S,UR,PB,DN,LIH,LIL,XH,XL,LF,LH,LL,YH,YL,YF,YA,AC,SA):
    f=s_ref[0]; blk=s_ref[1]; sb=s_ref[2]
    loads=[pltpu.make_async_copy(g_hbm.at[0,:,pl.ds(0,16)],g_ref.at[0,:,pl.ds(0,16)],sem.at[0]),
        pltpu.make_async_copy(g_hbm.at[0,:,pl.ds(16,24)],g_ref.at[0,:,pl.ds(16,24)],sem.at[1]),
        pltpu.make_async_copy(g_hbm.at[pl.ds(1,3)],g_ref.at[pl.ds(1,3)],sem.at[2]),
        pltpu.make_async_copy(c_hbm,c_ref,sem.at[3])]
    for cp in loads: cp.start()
    loads[0].wait()
    lane=lax.broadcasted_iota(jnp.int32,(128,128),1); row=lax.broadcasted_iota(jnp.int32,(128,128),0)
    eye=jnp.where(lane==row,1.0,0.0)
    def lterm(I,J,K,t):
        q=BLK[(I,K)]; w=BLK[(J,K)]
        return nt3(LH[q,rws(t),:],LL[q,rws(t),:],LH[w],LL[w])
    def yterm(J,K,t):
        w=BLK[(J,K)]
        return nt3(YH[K,rws(t),:],YL[K,rws(t),:],LH[w],LL[w])
    def xmul(acc,h):
        n=256*h+256
        ah,al=split(acc[:,:n])
        return nt3(ah,al,XH[256*h:n,:n],XL[256*h:n,:n])
    def psolve(I,J,t):
        acc=gtile(g_ref,I,J,t) if J==0 else AC[AX[(I,J)],rws(t),:]
        q=BLK[(I,J)]
        for h in range(2):
            p=xmul(acc,h)
            col=slice(256*h,256*h+256)
            LF[tri(I,J),rws(t),col]=p
            hi,lo=split(p)
            LH[q,rws(t),col]=hi; LL[q,rws(t),col]=lo
    def ysolve(J,t):
        acc=c_ref[0,rws(t),:] if J==0 else YA[J-1,rws(t),:]
        for h in range(2):
            p=xmul(acc,h)
            col=slice(256*h,256*h+256)
            YF[J,rws(t),col]=p
            if J<3:
                hi,lo=split(p)
                YH[J,rws(t),col]=hi; YL[J,rws(t),col]=lo
    def pupd(I,J,K,t):
        a=AX[(I,J)]
        v=gtile(g_ref,I,J,t) if K==0 else AC[a,rws(t),:]
        AC[a,rws(t),:]=v-lterm(I,J,K,t)
    def yupd(J,K,t):
        v=c_ref[J,rws(t),:] if K==0 else YA[J-1,rws(t),:]
        YA[J-1,rws(t),:]=v-yterm(J,K,t)
    def supd(J,K,t):
        v=gtile(g_ref,J,J,t) if K==0 else SA[J-2,rws(t),:]
        SA[J-2,rws(t),:]=v-lterm(J,J,K,t)
    T=functools.partial
    SIDE={(1,0):[(psolve,2,0),(psolve,3,0),(ysolve,0)],
          (1,1):[(pupd,2,1,0),(pupd,3,1,0),(yupd,1,0),(supd,2,0)],
          (2,0):[(psolve,3,1),(ysolve,1),(pupd,3,2,0),(yupd,2,0)],
          (2,1):[(pupd,3,2,1),(yupd,2,1),(supd,3,0),(supd,3,1)],
          (3,0):[(ysolve,2),(yupd,3,0),(yupd,3,1)],
          (3,1):[(yupd,3,2)]}
    for J in range(4):
        LIH[...]=jnp.zeros((128,128),BF); LIL[...]=jnp.zeros((128,128),BF)
        @pl.loop(0,2)
        def _(t):
            acc=gtile(g_ref,J,J,t) if J<2 else SA[J-2,rws(t),:]
            if J>0: acc=acc-lterm(J,J,J-1,t)
            for u in range(2):
                for c in range(4):
                    S[2*t+u,c]=acc[128*u:128*u+128,128*c:128*c+128]
        DN[...]=S[0,0]
        for half in range(2):
            @pl.loop(2*half,2*half+2)
            def _(b):
                prev=jnp.maximum(b-1,0)
                hold={}
                def d_ur():
                    rr=jnp.concatenate([jnp.where(prev==c,eye,S[prev,c]) for c in range(4)],axis=1)
                    rh,rl=split(rr)
                    ur=nn3(LIH[...],LIL[...],rh,rl)
                    for c in range(4):
                        UR[prev,c]=jnp.where(c<=prev,ur[:,128*c:128*c+128],0.0)
                    hold['u']=split(ur)
                def d_p(i):
                    ph,plo=split(S[i,prev])
                    p=jnp.where(prev<i,nt3(ph,plo,LIH[...],LIL[...]),0.0)
                    PB[i,prev]=jnp.where(prev<i,p,PB[i,prev])
                    S[i,prev]=jnp.where((prev<i)&(b>0),0.0,S[i,prev])
                    hold[i]=split(p)
                def d_s(i):
                    d=nn3(*hold[i],*hold['u'])
                    for c in range(4):
                        S[i,c]=S[i,c]-d[:,128*c:128*c+128]
                D=DN[...]
                side=[d_ur]+[T(d_p,i) for i in range(1,4)]+[T(d_s,i) for i in range(1,4)]
                side+=[T(w[0],*w[1:],b-2*half) for w in SIDE.get((J,half),[])]
                us,ls=diagC([D[8*k:8*k+8] for k in range(16)],side)
                li=jnp.concatenate(ls,axis=0)
                lh,ll=split(li)
                nx=jnp.minimum(b+1,3)
                ph,plo=split(S[nx,b])
                p=nt3(ph,plo,lh,ll)
                ph,plo=split(p)
                DN[...]=S[nx,nx]-nt3(ph,plo,ph,plo)
                LIH[...]=lh; LIL[...]=ll
                PB[b,b]=jnp.concatenate(us,axis=0).T
        rr=jnp.concatenate([S[3,c] for c in range(3)]+[eye],axis=1)
        rh,rl=split(rr)
        ur=nn3(LIH[...],LIL[...],rh,rl)
        for b in range(4):
            x=ur if b==3 else jnp.concatenate([UR[b,c] for c in range(4)],axis=1)
            h,l=split(x)
            XH[128*b:128*b+128,:]=h; XL[128*b:128*b+128,:]=l
            for c in range(4):
                LF[tri(J,J),128*b:128*b+128,128*c:128*c+128]=PB[b,c] if c<=b else jnp.zeros((128,128),F)
        if J==0:
            for cp in loads[1:]: cp.wait()
        if J<3:
            @pl.loop(0,2)
            def _(t): psolve(J+1,J,t)
    @pl.when(f==3)
    def _():
        @pl.loop(0,2)
        def _(t): ysolve(3,t)
    y_ref[...]=YF[f]
    ix=blk*(blk+1)//2+f
    f_ref[...]=jnp.where(blk>=f,LF[jnp.minimum(ix,9),pl.ds(pl.multiple_of(64*sb,64),64),:],0.0)
def k3call(s,g,c):
    V=pltpu.VMEM
    return pl.pallas_call(k3,out_shape=[jax.ShapeDtypeStruct((512,512),F),jax.ShapeDtypeStruct((64,512),F)],
        in_specs=[pl.BlockSpec(memory_space=pltpu.SMEM),pl.BlockSpec(memory_space=pl.ANY),pl.BlockSpec(memory_space=pl.ANY)],
        out_specs=[pl.BlockSpec(memory_space=V)]*2,
        scratch_shapes=[V((4,32,40,512),F),V((4,512,512),F),pltpu.SemaphoreType.DMA((4,)),V((4,4,128,128),F),V((4,4,128,128),F),V((4,4,128,128),F),V((128,128),F),V((128,128),BF),V((128,128),BF),V((512,512),BF),V((512,512),BF),V((10,512,512),F),
            V((6,512,512),BF),V((6,512,512),BF),V((3,512,512),BF),V((3,512,512),BF),V((4,512,512),F),V((3,512,512),F),V((3,512,512),F),V((2,512,512),F)],
        compiler_params=pltpu.CompilerParams(vmem_limit_bytes=60*2**20))(s,g,c)


MESH = pl.DeviceIdType.MESH


def remote(src, dst, send, recv, rows, feat):
    return pltpu.make_async_remote_copy(
        src_ref=src, dst_ref=dst, send_sem=send, recv_sem=recv,
        device_id=(rows, feat), device_id_type=MESH,
    )


def greet(peers):
    barrier = pltpu.get_barrier_semaphore()
    for rows, feat in peers:
        pl.semaphore_signal(barrier, inc=1, device_id=(rows, feat), device_id_type=MESH)
    pl.semaphore_wait(barrier, len(peers))


def gather_kernel(slab, c, m, sy, sz, sx, own, s_send, s_recv, m_send, m_recv, x_send, x_recv, b_send, b_recv, f_send, f_recv):
    r = lax.axis_index("rows")
    f = lax.axis_index("feat")
    core = f % 2
    side = f // 2
    sib = 2 * side + 1 - core
    opp = 2 * (1 - side) + core
    z, xh, y = r // 8, (r // 4) % 2, r % 4
    along_y = [(z * 2 + xh) * 4 + (y + d) % 4 for d in range(1, 4)]
    along_z = [(((z + d) % 4) * 2 + xh) * 4 + y for d in range(1, 4)]
    along_x = [(z * 2 + 1 - xh) * 4 + y]
    greet([(p, f) for p in along_y + along_z + along_x] + [(r, (f + d) % 4) for d in range(1, 4)])
    across = []
    for q in range(8):
        part = pl.ds(64 * q, 64)
        cp = remote(slab.at[part], c.at[f, part], x_send.at[q], x_recv.at[q], r, opp)
        cp.start()
        across.append(cp)
    beside = remote(slab, c.at[f], b_send, b_recv, r, sib)
    beside.start()
    keep = pltpu.make_async_copy(slab, c.at[f], own)
    keep.start()
    total = jnp.sum(slab[...], axis=0, keepdims=True)
    sent = []
    k = 0
    for box, at, peers in ((sy, y, along_y), (sz, z, along_z), (sx, xh, along_x)):
        box[at] = total
        group = []
        for to in peers:
            cp = remote(box.at[at], box.at[at], s_send.at[k], s_recv.at[k], to, f)
            cp.start()
            group.append(cp)
            k += 1
        for cp in group:
            cp.wait_recv()
        total = jnp.sum(box[...], axis=0)
        sent += group
    m[f] = total * (1.0 / 16384.0)
    shared = []
    for d in range(1, 4):
        cp = remote(m.at[f], m.at[f], m_send.at[d], m_recv.at[d], r, (f + d) % 4)
        cp.start()
        shared.append(cp)
    passed = []
    for q in range(8):
        part = pl.ds(64 * q, 64)
        across[q].wait_recv()
        cp = remote(c.at[opp, part], c.at[opp, part], f_send.at[q], f_recv.at[q], r, sib)
        cp.start()
        passed.append(cp)
    for cp in sent + across:
        cp.wait_send()
    for cp in shared + passed + [beside, keep]:
        cp.wait()


def gather(slab):
    D = pltpu.SemaphoreType.DMA
    V = pltpu.VMEM
    return pl.pallas_call(
        gather_kernel,
        out_shape=[jax.ShapeDtypeStruct((4, 512, 512), F), jax.ShapeDtypeStruct((4, 1, 512), F)],
        in_specs=[pl.BlockSpec(memory_space=V)],
        out_specs=[pl.BlockSpec(memory_space=V)] * 2,
        scratch_shapes=[V((4, 1, 512), F), V((4, 1, 512), F), V((2, 1, 512), F), D(()), D((7,)), D((7,)), D((4,)), D((4,)), D((8,)), D((8,)), D(()), D(()), D((8,)), D((8,))],
        compiler_params=pltpu.CompilerParams(collective_id=1, has_side_effects=True, vmem_limit_bytes=24 * 2**20),
    )(slab)


PIECE = ((0, 16), (16, 16), (32, 8))
ORDER = (("y", "z", "x"), ("z", "x", "y"), ("x", "y", "z"))


def reduce_kernel(parts, g, *scr):
    boxes = [[scr[12 * stage + 6 * q : 12 * stage + 6 * q + 6] for q in range(2)] for stage in range(2)]
    r1 = scr[24:26]
    r2, x_in, mine, p_send, p_recv, own, a_send, a_recv, c_send, c_recv = scr[26:]
    r = lax.axis_index("rows")
    f = lax.axis_index("feat")
    core = f % 2
    at = {"z": r // 8, "x": 2 * ((r // 4) % 2) + f // 2, "y": r % 4}
    half = at["x"] // 2

    def place(pos, cr):
        return (pos["z"] * 2 + pos["x"] // 2) * 4 + pos["y"], (pos["x"] % 2) * 2 + cr

    def moved(dim, by):
        pos = dict(at)
        pos[dim] = (at[dim] + by + 4) % 4
        return pos

    sib = place(at, 1 - core)
    def ring(dim, by):
        return place(moved(dim, by), core)

    greet([ring("y", 1), ring("y", -1), ring("z", 1), ring("z", -1), ring("x", 2), ring("x", 1), ring("x", -1), sib])
    first_dim = ("y", "z")
    sent = []

    def chunk(q, t, lo, n):
        lanes = pl.ds(256 * q + lo, n)
        return parts.at[:, :, t, :, lanes] if q == 0 else parts.at[t, :, :, :, lanes]

    def rest(q, t, lo, n):
        lanes = pl.ds(lo, n)
        return r1[0].at[t, :, :, lanes] if q == 0 else r1[1].at[:, t, :, lanes]

    def go(src, dst, k, to):
        cp = remote(src, dst, p_send.at[k], p_recv.at[k], *to)
        cp.start()
        sent.append(cp)
        return cp

    def idx(dim, by):
        return (at[dim] + by + 4) % 4

    for stage in range(2):
        get = chunk if stage == 0 else rest
        dims = first_dim if stage == 0 else first_dim[::-1]
        base = 10 * stage
        near = []
        for q in range(2):
            dim = dims[q]
            far = idx(dim, 2)
            near.append((
                go(get(q, far, 0, 128), boxes[stage][q][0], base + 4 * q, ring(dim, 1)),
                go(get(q, far, 128, 128), boxes[stage][q][1], base + 4 * q + 1, ring(dim, -1)),
            ))
        last = []
        for q in range(2):
            dim = dims[q]
            pair = []
            for way, by in enumerate((1, -1)):
                near[q][way].wait_recv()
                dst = boxes[stage][q][2 + way]
                lo = 128 * way
                dst[..., lo : lo + 128] = get(q, idx(dim, by), lo, 128)[...] + boxes[stage][q][way][...]
                other = 128 - lo
                dst[..., other : other + 128] = get(q, idx(dim, by), other, 128)[...]
                pair.append(go(dst, boxes[stage][q][4 + way], base + 4 * q + 2 + way, ring(dim, by)))
            last.append(pair)
        for q in range(2):
            dim = dims[q]
            for cp in last[q]:
                cp.wait_recv()
            res = get(q, at[dim], 0, 256)[...] + boxes[stage][q][4][...] + boxes[stage][q][5][...]
            if stage == 1:
                r2[q] = res
            else:
                r1[q][...] = res
    swap = [go(r2.at[q, 1 - half], x_in.at[q], 18 + q, ring("x", 2)) for q in range(2)]
    for q in range(2):
        swap[q].wait_recv()
        mine[:, 256 * q : 256 * q + 256] = r2[q, half] + x_in[q]

    def view(ref, piece, pos, full, lanes=(0, 512)):
        a, n = PIECE[piece]
        every = pl.ds(0, 4)
        two = pl.ds(0, 2)
        xl = two if "x" in full else pos["x"] % 2
        xh = two if "x" in full else pos["x"] // 2
        zz = every if "z" in full else pos["z"]
        yy = every if "y" in full else pos["y"]
        return ref.at[xl, core, zz, xh, yy, pl.ds(a, n), pl.ds(lanes[0], lanes[1])]

    pending = []
    count = [0]

    def pass_on(piece, pos, full):
        k = count[0]
        count[0] += 1
        v = view(g, piece, pos, full)
        cp = remote(v, v, c_send.at[k], c_recv.at[k], *sib)
        cp.start()
        pending.append(cp)

    for p in range(3):
        a, n = PIECE[p]
        cp = pltpu.make_async_copy(mine.at[pl.ds(a, n)], view(g, p, at, ()), own.at[p])
        cp.start()
        cp.wait()
    for s in range(3):
        first = []
        for p in range(3):
            dim = ORDER[p][s]
            full = ORDER[p][:s]
            v = view(g, p, at, full)
            pair = []
            for way, by in enumerate((1, -1)):
                k = (p * 3 + s) * 4 + way
                cp = remote(v, v, a_send.at[k], a_recv.at[k], *place(moved(dim, by), core))
                cp.start()
                pair.append(cp)
            first.append(pair)
            if s == 0:
                pass_on(p, at, ())
        second = []
        for p in range(3):
            dim = ORDER[p][s]
            full = ORDER[p][:s]
            pair = []
            for way, by in enumerate((1, -1)):
                first[p][way].wait_recv()
                k = (p * 3 + s) * 4 + 2 + way
                v = view(g, p, moved(dim, -by), full, (256 * way, 256))
                cp = remote(v, v, a_send.at[k], a_recv.at[k], *place(moved(dim, by), core))
                cp.start()
                pair.append(cp)
            second.append(pair)
            for by in (-1, 1):
                pass_on(p, moved(dim, by), full)
        for p in range(3):
            for cp in second[p]:
                cp.wait_recv()
            pass_on(p, moved(ORDER[p][s], 2), ORDER[p][:s])
            for cp in first[p] + second[p]:
                cp.wait_send()
    for cp in pending:
        cp.wait()
    for cp in sent:
        cp.wait_send()


def reduce_gather(parts):
    D = pltpu.SemaphoreType.DMA
    V = pltpu.VMEM
    lanes = (128, 128, 256, 256, 256, 256)
    scratch = [V((4, 2, 40, n), F) for n in lanes] + [V((2, 4, 40, n), F) for n in lanes]
    scratch += [V((2, 40, n), F) for n in lanes + lanes]
    scratch += [V((4, 2, 40, 256), F), V((2, 4, 40, 256), F), V((2, 2, 40, 256), F), V((2, 40, 256), F), V((40, 512), F)]
    scratch += [D((20,)), D((20,)), D((3,)), D((36,)), D((36,)), D((30,)), D((30,))]
    return pl.pallas_call(
        reduce_kernel,
        out_shape=jax.ShapeDtypeStruct((2, 2, 4, 2, 4, 40, 512), F),
        in_specs=[pl.BlockSpec(memory_space=V)],
        out_specs=pl.BlockSpec(memory_space=pl.ANY),
        scratch_shapes=scratch,
        compiler_params=pltpu.CompilerParams(collective_id=2, has_side_effects=True, vmem_limit_bytes=24 * 2**20),
    )(parts.reshape(4, 2, 4, 40, 512))


def dot_t(a, b):
    return lax.dot_general(
        a, b, (((0,), (0,)), ((), ())), precision=lax.Precision.HIGHEST, preferred_element_type=F
    )


def per_device(slab, cov_old):
    n_rows = lax.axis_size("rows")
    r = lax.axis_index("rows")
    f = lax.axis_index("feat")
    rows_dev, width = slab.shape
    total = rows_dev * n_rows
    blk = r // 8
    sub = r % 8
    raw, means = gather(slab)
    c = raw - means
    pick = lambda i: lax.dynamic_index_in_dim(c, i, 0, keepdims=False)
    o_row = jnp.minimum(f + 1, 3)
    o_col = jnp.where(f < 3, f, 0)
    h_row = jnp.where(f < 2, f + 2, f)
    h_col = jnp.where(f < 2, f, f - 2)
    h_low = jnp.where(f < 2, 0, 256)
    left_h = lax.dynamic_slice_in_dim(pick(h_row), h_low, 256, 1)
    base = lax.dynamic_update_slice_in_dim(jnp.zeros((512, 512), F), cov_old, 64 * sub, 0)
    base_t = base.T
    zero = jnp.zeros((), F)
    centered = pick(f)
    d = dot_t(centered, centered) / total + jnp.where(blk == f, base, zero)
    o = dot_t(pick(o_row), pick(o_col)) / total
    o += jnp.where(f < 3, jnp.where(blk == f + 1, base, zero), jnp.where(blk == 0, base_t, zero))
    h = dot_t(left_h, pick(h_col)) / total
    h += jnp.where(
        f < 2,
        jnp.where(blk == f + 2, base[:256], zero),
        jnp.where(blk == f - 2, base_t[256:], zero),
    )
    parts = jnp.concatenate(
        [d.reshape(32, 16, 512), o.reshape(32, 16, 512), h.reshape(32, 8, 512)], axis=1
    )
    g = reduce_gather(parts).reshape(4, 32, 40, 512)
    s = jnp.stack([f, blk, sub]).astype(jnp.int32)
    y, fac = k3call(s, g, c)
    return (y, fac)


def solution(mesh):
    placed = (P("rows", "feat"), P("rows", "feat"))
    return jax.shard_map(
        per_device, mesh=mesh, in_specs=placed, out_specs=placed, check_vma=False
    )
```

```python
import functools
import jax
import jax.numpy as jnp
from jax import lax
from jax.experimental import pallas as pl
from jax.experimental.pallas import tpu as pltpu
from jax.sharding import PartitionSpec as P

F = jnp.float32
BF = jnp.bfloat16


def sbc(x, j):
    return jnp.broadcast_to(x[j : j + 1, :], (8, 128))


def lbc(x, c):
    return jnp.broadcast_to(x[:, c : c + 1], (8, 128))


BF=jnp.bfloat16
def split(x):
    h=x.astype(BF); return h,(x-h.astype(F)).astype(BF)
def mm(a,b): return jnp.dot(a,b,preferred_element_type=F)
def diagC(W,side=(),vr=2):
    W=list(W)
    lane=lax.broadcasted_iota(jnp.int32,(8,128),1); sub=lax.broadcasted_iota(jnp.int32,(8,128),0)
    us=[];ls=[]
    C=[lbc(W[0],j) for j in range(8)]
    for k in range(16):
        for q in side[k::16]: q()
        R=W[k]
        g=8*k
        ing=(lane>=g)&(lane<g+8)
        X=jnp.where(ing,jnp.where(lane-g==sub,1.0,0.0),R); V=R
        FX=X; FV=V
        pv=jnp.ones((8,128),F)
        nxt=k<15
        if nxt:
            Q=[lbc(W[k+1],g+c) for c in range(16)]
            Q0=Q[:8]
        for j in range(0,8,2):
            a=sbc(C[j],j); b=sbc(C[j],j+1); d=sbc(C[j+1],j+1)
            det=a*d-b*b
            rd=1.0/det
            c0=C[j]; c1=C[j+1]
            s0=sub==j; s1=sub==j+1; sp=s0|s1
            n0=jnp.where(s0,-d,jnp.where(s1,b,c0*d-c1*b)); n1=jnp.where(s0,b,jnp.where(s1,-a,c1*a-c0*b))
            m0=n0*rd; m1=n1*rd
            if nxt:
                q0=Q[j]; q1=Q[j+1]
                h0=(q0*d-q1*b)*rd; h1=(q1*a-q0*b)*rd
            def upd(q):
                r0=sbc(q,j); r1=sbc(q,j+1)
                return jnp.where(sp,0.0,q)-(m0*r0+m1*r1), r0, r1
            for c in range(j+2,8):
                C[c],r0,r1=upd(C[c])
                if nxt: Q[c]=Q[c]-(h0*r0+h1*r1)
            if nxt:
                for c in range(8):
                    Q[8+c]=Q[8+c]-(h0*sbc(q0,c)+h1*sbc(q1,c))
            ba=b/a
            X,r0,r1=upd(X)
            FX=jnp.where(s0,r0,jnp.where(s1,r1-ba*r0,FX))
            V,r0,r1=upd(V)
            FV=jnp.where(s0,r0,jnp.where(s1,r1-ba*r0,FV))
            pv=jnp.where(s0,a,jnp.where(s1,d-ba*b,pv))
        Z=X; rs=lax.rsqrt(pv)
        us.append(jnp.where(lane>=g+sub,FV*rs,0.0)); ls.append(jnp.where(lane<=g+sub,FX*rs,0.0))
        zb=[sbc(Z,j) for j in range(8)]
        if nxt: C=Q[8:]
        for i in range(k+1,min(k+1+vr,16)):
            acc=jnp.where(ing,0.0,W[i])
            for j in range(8):
                acc=acc-(Q0[j] if i==k+1 else lbc(W[i],g+j))*zb[j]
            W[i]=acc
        lo=k+1+vr
        if lo<16:
            Wt=jnp.concatenate(W[lo:],axis=0); wh,wl=split(Wt)
            zz=[jnp.zeros((8*k,128),F)] if k else []
            Zf=jnp.concatenate(zz+[Z,jnp.zeros((120-8*k,128),F)],axis=0)
            zh,zl=split(Zf)
            D=mm(wh,zh)+(mm(wh,zl)+mm(wl,zh))
            for i in range(lo,16):
                W[i]=jnp.where(ing,0.0,W[i])-D[8*(i-lo):8*(i-lo)+8]
    return us,ls

BLK={(1,0):0,(2,0):1,(3,0):2,(2,1):3,(3,1):4,(3,2):5}
AX={(2,1):0,(3,1):1,(3,2):2}
def tri(i,j): return i*(i+1)//2+j
def nt(a,b): return lax.dot_general(a,b,(((1,),(1,)),((),())),preferred_element_type=F)
def nt3(ah,al,bh,bl): return nt(ah,bh)+(nt(ah,bl)+nt(al,bh))
def nn3(ah,al,bh,bl): return mm(ah,bh)+(mm(ah,bl)+mm(al,bh))
def gtile(g_ref,I,J,t):
    if I==J: return g_ref[J,pl.ds(16*t,16),0:16,:].reshape(256,512)
    if (I,J)==(3,0): return g_ref[3,pl.ds(16*t,16),16:32,:].reshape(256,512)
    if I==J+1: return g_ref[J,pl.ds(16*t,16),16:32,:].reshape(256,512)
    return g_ref[J+2*t,:,32:40,:].reshape(256,512)
def rws(t): return pl.ds(pl.multiple_of(256*t,256),256)
def k3(s_ref,g_hbm,c_hbm,y_ref,f_ref,g_ref,c_ref,sem,S,UR,PB,DN,LIH,LIL,XH,XL,LF,LH,LL,YH,YL,YF,YA,AC,SA):
    f=s_ref[0]; blk=s_ref[1]; sb=s_ref[2]
    loads=[pltpu.make_async_copy(g_hbm.at[0,:,pl.ds(0,16)],g_ref.at[0,:,pl.ds(0,16)],sem.at[0]),
        pltpu.make_async_copy(g_hbm.at[0,:,pl.ds(16,24)],g_ref.at[0,:,pl.ds(16,24)],sem.at[1]),
        pltpu.make_async_copy(g_hbm.at[pl.ds(1,3)],g_ref.at[pl.ds(1,3)],sem.at[2]),
        pltpu.make_async_copy(c_hbm,c_ref,sem.at[3])]
    for cp in loads: cp.start()
    loads[0].wait()
    lane=lax.broadcasted_iota(jnp.int32,(128,128),1); row=lax.broadcasted_iota(jnp.int32,(128,128),0)
    eye=jnp.where(lane==row,1.0,0.0)
    def lterm(I,J,K,t):
        q=BLK[(I,K)]; w=BLK[(J,K)]
        return nt3(LH[q,rws(t),:],LL[q,rws(t),:],LH[w],LL[w])
    def yterm(J,K,t):
        w=BLK[(J,K)]
        return nt3(YH[K,rws(t),:],YL[K,rws(t),:],LH[w],LL[w])
    def xmul(acc,h):
        n=256*h+256
        ah,al=split(acc[:,:n])
        return nt3(ah,al,XH[256*h:n,:n],XL[256*h:n,:n])
    def psolve(I,J,t):
        acc=gtile(g_ref,I,J,t) if J==0 else AC[AX[(I,J)],rws(t),:]
        q=BLK[(I,J)]
        for h in range(2):
            p=xmul(acc,h)
            col=slice(256*h,256*h+256)
            LF[tri(I,J),rws(t),col]=p
            hi,lo=split(p)
            LH[q,rws(t),col]=hi; LL[q,rws(t),col]=lo
    def ysolve(J,t):
        acc=c_ref[0,rws(t),:] if J==0 else YA[J-1,rws(t),:]
        for h in range(2):
            p=xmul(acc,h)
            col=slice(256*h,256*h+256)
            YF[J,rws(t),col]=p
            if J<3:
                hi,lo=split(p)
                YH[J,rws(t),col]=hi; YL[J,rws(t),col]=lo
    def pupd(I,J,K,t):
        a=AX[(I,J)]
        v=gtile(g_ref,I,J,t) if K==0 else AC[a,rws(t),:]
        AC[a,rws(t),:]=v-lterm(I,J,K,t)
    def yupd(J,K,t):
        v=c_ref[J,rws(t),:] if K==0 else YA[J-1,rws(t),:]
        YA[J-1,rws(t),:]=v-yterm(J,K,t)
    def supd(J,K,t):
        v=gtile(g_ref,J,J,t) if K==0 else SA[J-2,rws(t),:]
        SA[J-2,rws(t),:]=v-lterm(J,J,K,t)
    T=functools.partial
    SIDE={(1,0):[(psolve,2,0),(psolve,3,0),(ysolve,0)],
          (1,1):[(pupd,2,1,0),(pupd,3,1,0),(yupd,1,0),(supd,2,0)],
          (2,0):[(psolve,3,1),(ysolve,1),(pupd,3,2,0),(yupd,2,0)],
          (2,1):[(pupd,3,2,1),(yupd,2,1),(supd,3,0),(supd,3,1)],
          (3,0):[(ysolve,2),(yupd,3,0),(yupd,3,1)],
          (3,1):[(yupd,3,2)]}
    for J in range(4):
        LIH[...]=jnp.zeros((128,128),BF); LIL[...]=jnp.zeros((128,128),BF)
        @pl.loop(0,2)
        def _(t):
            acc=gtile(g_ref,J,J,t) if J<2 else SA[J-2,rws(t),:]
            if J>0: acc=acc-lterm(J,J,J-1,t)
            for u in range(2):
                for c in range(4):
                    S[2*t+u,c]=acc[128*u:128*u+128,128*c:128*c+128]
        DN[...]=S[0,0]
        for half in range(2):
            @pl.loop(2*half,2*half+2)
            def _(b):
                prev=jnp.maximum(b-1,0)
                hold={}
                def d_ur():
                    rr=jnp.concatenate([jnp.where(prev==c,eye,S[prev,c]) for c in range(4)],axis=1)
                    rh,rl=split(rr)
                    ur=nn3(LIH[...],LIL[...],rh,rl)
                    for c in range(4):
                        UR[prev,c]=jnp.where(c<=prev,ur[:,128*c:128*c+128],0.0)
                    hold['u']=split(ur)
                def d_p(i):
                    ph,plo=split(S[i,prev])
                    p=jnp.where(prev<i,nt3(ph,plo,LIH[...],LIL[...]),0.0)
                    PB[i,prev]=jnp.where(prev<i,p,PB[i,prev])
                    S[i,prev]=jnp.where((prev<i)&(b>0),0.0,S[i,prev])
                    hold[i]=split(p)
                def d_s(i):
                    d=nn3(*hold[i],*hold['u'])
                    for c in range(4):
                        S[i,c]=S[i,c]-d[:,128*c:128*c+128]
                D=DN[...]
                side=[d_ur]+[T(d_p,i) for i in range(1,4)]+[T(d_s,i) for i in range(1,4)]
                side+=[T(w[0],*w[1:],b-2*half) for w in SIDE.get((J,half),[])]
                us,ls=diagC([D[8*k:8*k+8] for k in range(16)],side,16)
                li=jnp.concatenate(ls,axis=0)
                lh,ll=split(li)
                nx=jnp.minimum(b+1,3)
                ph,plo=split(S[nx,b])
                p=nt3(ph,plo,lh,ll)
                ph,plo=split(p)
                DN[...]=S[nx,nx]-nt3(ph,plo,ph,plo)
                LIH[...]=lh; LIL[...]=ll
                PB[b,b]=jnp.concatenate(us,axis=0).T
        rr=jnp.concatenate([S[3,c] for c in range(3)]+[eye],axis=1)
        rh,rl=split(rr)
        ur=nn3(LIH[...],LIL[...],rh,rl)
        for b in range(4):
            x=ur if b==3 else jnp.concatenate([UR[b,c] for c in range(4)],axis=1)
            h,l=split(x)
            XH[128*b:128*b+128,:]=h; XL[128*b:128*b+128,:]=l
            for c in range(4):
                LF[tri(J,J),128*b:128*b+128,128*c:128*c+128]=PB[b,c] if c<=b else jnp.zeros((128,128),F)
        if J==0:
            for cp in loads[1:]: cp.wait()
        if J<3:
            @pl.loop(0,2)
            def _(t): psolve(J+1,J,t)
    @pl.when(f==3)
    def _():
        @pl.loop(0,2)
        def _(t): ysolve(3,t)
    y_ref[...]=YF[f]
    ix=blk*(blk+1)//2+f
    f_ref[...]=jnp.where(blk>=f,LF[jnp.minimum(ix,9),pl.ds(pl.multiple_of(64*sb,64),64),:],0.0)
def k3call(s,g,c):
    V=pltpu.VMEM
    return pl.pallas_call(k3,out_shape=[jax.ShapeDtypeStruct((512,512),F),jax.ShapeDtypeStruct((64,512),F)],
        in_specs=[pl.BlockSpec(memory_space=pltpu.SMEM),pl.BlockSpec(memory_space=pl.ANY),pl.BlockSpec(memory_space=pl.ANY)],
        out_specs=[pl.BlockSpec(memory_space=V)]*2,
        scratch_shapes=[V((4,32,40,512),F),V((4,512,512),F),pltpu.SemaphoreType.DMA((4,)),V((4,4,128,128),F),V((4,4,128,128),F),V((4,4,128,128),F),V((128,128),F),V((128,128),BF),V((128,128),BF),V((512,512),BF),V((512,512),BF),V((10,512,512),F),
            V((6,512,512),BF),V((6,512,512),BF),V((3,512,512),BF),V((3,512,512),BF),V((4,512,512),F),V((3,512,512),F),V((3,512,512),F),V((2,512,512),F)],
        compiler_params=pltpu.CompilerParams(vmem_limit_bytes=60*2**20))(s,g,c)


MESH = pl.DeviceIdType.MESH


def remote(src, dst, send, recv, rows, feat):
    return pltpu.make_async_remote_copy(
        src_ref=src, dst_ref=dst, send_sem=send, recv_sem=recv,
        device_id=(rows, feat), device_id_type=MESH,
    )


def greet(peers):
    barrier = pltpu.get_barrier_semaphore()
    for rows, feat in peers:
        pl.semaphore_signal(barrier, inc=1, device_id=(rows, feat), device_id_type=MESH)
    pl.semaphore_wait(barrier, len(peers))


def gather_kernel(slab, c, m, sy, sz, sx, own, s_send, s_recv, m_send, m_recv, x_send, x_recv, b_send, b_recv, f_send, f_recv):
    r = lax.axis_index("rows")
    f = lax.axis_index("feat")
    core = f % 2
    side = f // 2
    sib = 2 * side + 1 - core
    opp = 2 * (1 - side) + core
    z, xh, y = r // 8, (r // 4) % 2, r % 4
    along_y = [(z * 2 + xh) * 4 + (y + d) % 4 for d in range(1, 4)]
    along_z = [(((z + d) % 4) * 2 + xh) * 4 + y for d in range(1, 4)]
    along_x = [(z * 2 + 1 - xh) * 4 + y]
    greet([(p, f) for p in along_y + along_z + along_x] + [(r, (f + d) % 4) for d in range(1, 4)])
    across = []
    for q in range(8):
        part = pl.ds(64 * q, 64)
        cp = remote(slab.at[part], c.at[f, part], x_send.at[q], x_recv.at[q], r, opp)
        cp.start()
        across.append(cp)
    beside = remote(slab, c.at[f], b_send, b_recv, r, sib)
    beside.start()
    keep = pltpu.make_async_copy(slab, c.at[f], own)
    keep.start()
    total = jnp.sum(slab[...], axis=0, keepdims=True)
    sent = []
    k = 0
    for box, at, peers in ((sy, y, along_y), (sz, z, along_z), (sx, xh, along_x)):
        box[at] = total
        group = []
        for to in peers:
            cp = remote(box.at[at], box.at[at], s_send.at[k], s_recv.at[k], to, f)
            cp.start()
            group.append(cp)
            k += 1
        for cp in group:
            cp.wait_recv()
        total = jnp.sum(box[...], axis=0)
        sent += group
    m[f] = total * (1.0 / 16384.0)
    shared = []
    for d in range(1, 4):
        cp = remote(m.at[f], m.at[f], m_send.at[d], m_recv.at[d], r, (f + d) % 4)
        cp.start()
        shared.append(cp)
    passed = []
    for q in range(8):
        part = pl.ds(64 * q, 64)
        across[q].wait_recv()
        cp = remote(c.at[opp, part], c.at[opp, part], f_send.at[q], f_recv.at[q], r, sib)
        cp.start()
        passed.append(cp)
    for cp in sent + across:
        cp.wait_send()
    for cp in shared + passed + [beside, keep]:
        cp.wait()


def gather(slab):
    D = pltpu.SemaphoreType.DMA
    V = pltpu.VMEM
    return pl.pallas_call(
        gather_kernel,
        out_shape=[jax.ShapeDtypeStruct((4, 512, 512), F), jax.ShapeDtypeStruct((4, 1, 512), F)],
        in_specs=[pl.BlockSpec(memory_space=V)],
        out_specs=[pl.BlockSpec(memory_space=V)] * 2,
        scratch_shapes=[V((4, 1, 512), F), V((4, 1, 512), F), V((2, 1, 512), F), D(()), D((7,)), D((7,)), D((4,)), D((4,)), D((8,)), D((8,)), D(()), D(()), D((8,)), D((8,))],
        compiler_params=pltpu.CompilerParams(collective_id=1, has_side_effects=True, vmem_limit_bytes=24 * 2**20),
    )(slab)


PIECE = ((0, 16), (16, 16), (32, 8))
ORDER = (("y", "z", "x"), ("z", "x", "y"), ("x", "y", "z"))


def reduce_kernel(parts, g, *scr):
    boxes = [[scr[12 * stage + 6 * q : 12 * stage + 6 * q + 6] for q in range(2)] for stage in range(2)]
    r1 = scr[24:26]
    r2, x_in, mine, p_send, p_recv, own, a_send, a_recv, c_send, c_recv = scr[26:]
    r = lax.axis_index("rows")
    f = lax.axis_index("feat")
    core = f % 2
    at = {"z": r // 8, "x": 2 * ((r // 4) % 2) + f // 2, "y": r % 4}
    half = at["x"] // 2

    def place(pos, cr):
        return (pos["z"] * 2 + pos["x"] // 2) * 4 + pos["y"], (pos["x"] % 2) * 2 + cr

    def moved(dim, by):
        pos = dict(at)
        pos[dim] = (at[dim] + by + 4) % 4
        return pos

    sib = place(at, 1 - core)
    def ring(dim, by):
        return place(moved(dim, by), core)

    greet([ring("y", 1), ring("y", -1), ring("z", 1), ring("z", -1), ring("x", 2), ring("x", 1), ring("x", -1), sib])
    first_dim = ("y", "z")
    sent = []

    def chunk(q, t, lo, n):
        lanes = pl.ds(256 * q + lo, n)
        return parts.at[:, :, t, :, lanes] if q == 0 else parts.at[t, :, :, :, lanes]

    def rest(q, t, lo, n):
        lanes = pl.ds(lo, n)
        return r1[0].at[t, :, :, lanes] if q == 0 else r1[1].at[:, t, :, lanes]

    def go(src, dst, k, to):
        cp = remote(src, dst, p_send.at[k], p_recv.at[k], *to)
        cp.start()
        sent.append(cp)
        return cp

    def idx(dim, by):
        return (at[dim] + by + 4) % 4

    for stage in range(2):
        get = chunk if stage == 0 else rest
        dims = first_dim if stage == 0 else first_dim[::-1]
        base = 10 * stage
        near = []
        for q in range(2):
            dim = dims[q]
            far = idx(dim, 2)
            near.append((
                go(get(q, far, 0, 128), boxes[stage][q][0], base + 4 * q, ring(dim, 1)),
                go(get(q, far, 128, 128), boxes[stage][q][1], base + 4 * q + 1, ring(dim, -1)),
            ))
        last = []
        for q in range(2):
            dim = dims[q]
            pair = []
            for way, by in enumerate((1, -1)):
                near[q][way].wait_recv()
                dst = boxes[stage][q][2 + way]
                lo = 128 * way
                dst[..., lo : lo + 128] = get(q, idx(dim, by), lo, 128)[...] + boxes[stage][q][way][...]
                other = 128 - lo
                dst[..., other : other + 128] = get(q, idx(dim, by), other, 128)[...]
                pair.append(go(dst, boxes[stage][q][4 + way], base + 4 * q + 2 + way, ring(dim, by)))
            last.append(pair)
        for q in range(2):
            dim = dims[q]
            for cp in last[q]:
                cp.wait_recv()
            res = get(q, at[dim], 0, 256)[...] + boxes[stage][q][4][...] + boxes[stage][q][5][...]
            if stage == 1:
                r2[q] = res
            else:
                r1[q][...] = res
    swap = [go(r2.at[q, 1 - half], x_in.at[q], 18 + q, ring("x", 2)) for q in range(2)]
    for q in range(2):
        swap[q].wait_recv()
        mine[:, 256 * q : 256 * q + 256] = r2[q, half] + x_in[q]

    def view(ref, piece, pos, full, lanes=(0, 512)):
        a, n = PIECE[piece]
        every = pl.ds(0, 4)
        two = pl.ds(0, 2)
        xl = two if "x" in full else pos["x"] % 2
        xh = two if "x" in full else pos["x"] // 2
        zz = every if "z" in full else pos["z"]
        yy = every if "y" in full else pos["y"]
        return ref.at[xl, core, zz, xh, yy, pl.ds(a, n), pl.ds(lanes[0], lanes[1])]

    pending = []
    count = [0]

    def pass_on(piece, pos, full):
        k = count[0]
        count[0] += 1
        v = view(g, piece, pos, full)
        cp = remote(v, v, c_send.at[k], c_recv.at[k], *sib)
        cp.start()
        pending.append(cp)

    for p in range(3):
        a, n = PIECE[p]
        cp = pltpu.make_async_copy(mine.at[pl.ds(a, n)], view(g, p, at, ()), own.at[p])
        cp.start()
        cp.wait()
    for s in range(3):
        first = []
        for p in range(3):
            dim = ORDER[p][s]
            full = ORDER[p][:s]
            v = view(g, p, at, full)
            pair = []
            for way, by in enumerate((1, -1)):
                k = (p * 3 + s) * 4 + way
                cp = remote(v, v, a_send.at[k], a_recv.at[k], *place(moved(dim, by), core))
                cp.start()
                pair.append(cp)
            first.append(pair)
            if s == 0:
                pass_on(p, at, ())
        second = []
        for p in range(3):
            dim = ORDER[p][s]
            full = ORDER[p][:s]
            pair = []
            for way, by in enumerate((1, -1)):
                first[p][way].wait_recv()
                k = (p * 3 + s) * 4 + 2 + way
                v = view(g, p, moved(dim, -by), full, (256 * way, 256))
                cp = remote(v, v, a_send.at[k], a_recv.at[k], *place(moved(dim, by), core))
                cp.start()
                pair.append(cp)
            second.append(pair)
            for by in (-1, 1):
                pass_on(p, moved(dim, by), full)
        for p in range(3):
            for cp in second[p]:
                cp.wait_recv()
            pass_on(p, moved(ORDER[p][s], 2), ORDER[p][:s])
            for cp in first[p] + second[p]:
                cp.wait_send()
    for cp in pending:
        cp.wait()
    for cp in sent:
        cp.wait_send()


def reduce_gather(parts):
    D = pltpu.SemaphoreType.DMA
    V = pltpu.VMEM
    lanes = (128, 128, 256, 256, 256, 256)
    scratch = [V((4, 2, 40, n), F) for n in lanes] + [V((2, 4, 40, n), F) for n in lanes]
    scratch += [V((2, 40, n), F) for n in lanes + lanes]
    scratch += [V((4, 2, 40, 256), F), V((2, 4, 40, 256), F), V((2, 2, 40, 256), F), V((2, 40, 256), F), V((40, 512), F)]
    scratch += [D((20,)), D((20,)), D((3,)), D((36,)), D((36,)), D((30,)), D((30,))]
    return pl.pallas_call(
        reduce_kernel,
        out_shape=jax.ShapeDtypeStruct((2, 2, 4, 2, 4, 40, 512), F),
        in_specs=[pl.BlockSpec(memory_space=V)],
        out_specs=pl.BlockSpec(memory_space=pl.ANY),
        scratch_shapes=scratch,
        compiler_params=pltpu.CompilerParams(collective_id=2, has_side_effects=True, vmem_limit_bytes=56 * 2**20),
    )(parts.reshape(4, 2, 4, 40, 512))


def dot_t(a, b):
    return lax.dot_general(
        a, b, (((0,), (0,)), ((), ())), precision=lax.Precision.HIGH, preferred_element_type=F
    )


def per_device(slab, cov_old):
    n_rows = lax.axis_size("rows")
    r = lax.axis_index("rows")
    f = lax.axis_index("feat")
    rows_dev, width = slab.shape
    total = rows_dev * n_rows
    blk = r // 8
    sub = r % 8
    raw, means = gather(slab)
    c = raw - means
    pick = lambda i: lax.dynamic_index_in_dim(c, i, 0, keepdims=False)
    o_row = jnp.minimum(f + 1, 3)
    o_col = jnp.where(f < 3, f, 0)
    h_row = jnp.where(f < 2, f + 2, f)
    h_col = jnp.where(f < 2, f, f - 2)
    h_low = jnp.where(f < 2, 0, 256)
    left_h = lax.dynamic_slice_in_dim(pick(h_row), h_low, 256, 1)
    base = lax.dynamic_update_slice_in_dim(jnp.zeros((512, 512), F), cov_old, 64 * sub, 0)
    base_t = base.T
    zero = jnp.zeros((), F)
    centered = pick(f)
    d = dot_t(centered, centered) / total + jnp.where(blk == f, base, zero)
    o = dot_t(pick(o_row), pick(o_col)) / total
    o += jnp.where(f < 3, jnp.where(blk == f + 1, base, zero), jnp.where(blk == 0, base_t, zero))
    h = dot_t(left_h, pick(h_col)) / total
    h += jnp.where(
        f < 2,
        jnp.where(blk == f + 2, base[:256], zero),
        jnp.where(blk == f - 2, base_t[256:], zero),
    )
    parts = jnp.concatenate(
        [d.reshape(32, 16, 512), o.reshape(32, 16, 512), h.reshape(32, 8, 512)], axis=1
    )
    g = reduce_gather(parts).reshape(4, 32, 40, 512)
    s = jnp.stack([f, blk, sub]).astype(jnp.int32)
    y, fac = k3call(s, g, c)
    return (y, fac)


def solution(mesh):
    placed = (P("rows", "feat"), P("rows", "feat"))
    return jax.shard_map(
        per_device, mesh=mesh, in_specs=placed, out_specs=placed, check_vma=False
    )
```
